256 devices in a mesh: tensor: 8 (over z), vocab: 32 (over x, y, core).
Axes of the slice: x: 4, y: 4, z: 8, core: 2. Of those that a mesh axis runs over, the one named last changes fastest.
Arguments:
- activated_perceptron_values: bfloat16 [2, 64, 21504], P(None, None, 'tensor'), may hold values from -6 to 6
- contraction_matrix: bfloat16 [21504, 5376], P('tensor', 'vocab'), may hold values from -0.0390625 to 0.0390625
- posterior_layer_gain: float32 [5376], P('vocab'), may hold values from -2.5 to 2.5
- skip_connection_vector: bfloat16 [2, 64, 5376], P(None, None, 'vocab'), may hold values from -6 to 6
- closing_layer_gain: float32 [5376], P('vocab'), may hold values from -2.5 to 2.5
- lexicon_matrix: bfloat16 [262144, 5376], P(('tensor', 'vocab')), may hold values from -0.25 to 0.25
- softmax_warmth: float32 [2, 64], replicated, may hold values from 0.02 to 1
- prohibited_segment_ids: int32 [2, 64, 16], replicated, may hold values from 0 to 127
- prohibited_segment_total: int32 [2, 64], replicated, may hold values from 0 to 16, as said below
- subsequent_symbol_ids: int32 [64], replicated, may hold values from 0 to 262143
Outputs:
- log_probs: float32 [2, 64, 262144], P(None, None, ('tensor', 'vocab'))
The draws below stay inside these ranges and needn't reach their ends.
Inputs may be any that keep to these rules, and one draw needn't show every extreme that they name: `prohibited_segment_ids`: only the first prohibited_segment_total entries of a row's list count; ids may repeat. `prohibited_segment_total`: some row of each step uses all 16 slots.
All inputs are finite; a program needn't handle non-finite values.
Results may differ from the reference program's by a relative error of at most 0.00094.
Values may be sent and summed in bfloat16 or wider, within the bound.
A program may use at most 64 MiB of HBM per device.

```python
import math
import jax
import jax.numpy as jnp
import numpy as np
from jax import lax

D = 5376
FF = 21504
V = 262144
BLOCK = 2048
NB = 16
GENERATION_ITERS = 2
DRAWN_SEQUENCES = 64
BLOCKS = 128


def draw_prohibited_segment_total(key, part):
    key = jax.random.fold_in(key, 7)
    counts = jax.random.randint(key, (GENERATION_ITERS, DRAWN_SEQUENCES), 0, NB + 1)
    first_row = jnp.arange(DRAWN_SEQUENCES, dtype=jnp.int32)[None, :] == 0
    return jnp.where(first_row, NB, counts).astype(jnp.int32)


def with_ends(values, stream_key, least, top_value):
    longest = values.shape.index(max(values.shape))
    spots = []
    for shift in (0, 1):
        where = [jax.random.randint(jax.random.fold_in(stream_key, axis), (), 0, length) for axis, length in enumerate(values.shape)]
        where[longest] = (where[longest] + shift) % values.shape[longest]
        spots.append(tuple(where))
    return values.at[spots[0]].set(least).at[spots[1]].set(top_value)


def shard_levels(key, extent, cuts, low, top_value):
    level, own = 1.0, jax.random.fold_in(key, 6)
    for axis_at, blocks in cuts:
        steps = jnp.exp(jax.random.uniform(jax.random.fold_in(own, axis_at), (blocks,), jnp.float32, low / len(cuts), top_value / len(cuts)))
        level = level * jnp.repeat(steps, extent[axis_at] // blocks).reshape([-1 if axis == axis_at else 1 for axis in range(len(extent))])
    return level


def rank_table(count, slope):
    portions = [(1 << 20) // math.isqrt(standing ** slope) + 1 for standing in range(1, count + 1)]
    deviation = 1 + sum(portions) // (1 << 30)
    return np.cumsum(np.array([max(1, weight // deviation) for weight in portions]))


def skewed_ids(key, dims, number_of, slope):
    table = rank_table(number_of, slope)
    ticket = jax.random.randint(jax.random.fold_in(key, 1), dims, 0, int(table[number_of - 1]))
    standing = jnp.searchsorted(jnp.asarray(table, jnp.int32), ticket, side="right")
    return jax.random.permutation(jax.random.fold_in(key, 2), number_of)[standing].astype(jnp.int32)


def normal_values(rng, dims, width, bound, cuts=(), held_as=jnp.bfloat16):
    result = width * jax.random.normal(rng, dims, jnp.float32)
    if cuts:
        result = result * shard_levels(rng, dims, cuts, -0.22, 0.18)
    return jnp.clip(result, -bound, bound).astype(held_as)


def setup_inputs(seed: int = 0) -> dict:
    keys = jax.random.split(jax.random.key(seed), 11)
    return {
        "activated_perceptron_values": normal_values(keys[0], (GENERATION_ITERS, DRAWN_SEQUENCES, FF), 1.0, 6.0, ((2, 8),)),
        "contraction_matrix": normal_values(keys[1], (FF, D), FF ** -0.5, 0.0390625, ((0, 8), (1, 32))),
        "posterior_layer_gain": normal_values(keys[2], (D,), 0.5, 2.5, ((0, 32),), jnp.float32),
        "skip_connection_vector": normal_values(keys[3], (GENERATION_ITERS, DRAWN_SEQUENCES, D), 1.0, 6.0, ((2, 32),)),
        "closing_layer_gain": normal_values(keys[4], (D,), 0.5, 2.5, ((0, 32),), jnp.float32),
        "lexicon_matrix": normal_values(keys[5], (V, D), (D // 9) ** -0.5, 0.25, ((0, 256),)),
        "softmax_warmth": jnp.clip(jnp.exp(jax.random.uniform(keys[6], (GENERATION_ITERS, DRAWN_SEQUENCES), jnp.float32, math.log(0.02), math.log(1.0))), 0.02, 1.0),
        "prohibited_segment_ids": with_ends(skewed_ids(keys[7], (GENERATION_ITERS, DRAWN_SEQUENCES, NB), BLOCKS, 2), jax.random.fold_in(keys[7], 3), 0, BLOCKS - 1).astype(jnp.int32),
        "prohibited_segment_total": draw_prohibited_segment_total(jax.random.fold_in(keys[10], 71), 0),
        "subsequent_symbol_ids": with_ends(jax.random.randint(keys[9], (DRAWN_SEQUENCES,), 0, V), jax.random.fold_in(keys[9], 1), 0, V - 1).astype(jnp.int32),
    }


def reference(activated_perceptron_values, contraction_matrix, posterior_layer_gain, skip_connection_vector, closing_layer_gain, lexicon_matrix, softmax_warmth, prohibited_segment_ids, prohibited_segment_total, subsequent_symbol_ids):
    results = []
    block_ids = jnp.arange(BLOCKS, dtype=jnp.int32)
    slot_ids = jnp.arange(NB, dtype=jnp.int32)
    for generation_position in range(GENERATION_ITERS):
        projected = jnp.dot(activated_perceptron_values[generation_position], contraction_matrix, preferred_element_type=jnp.float32)
        postsq = lax.optimization_barrier(jnp.mean(projected * projected, axis=1, keepdims=True))
        summed = skip_connection_vector[generation_position].astype(jnp.float32) + projected * lax.rsqrt(postsq + 1e-06) * (1.0 + posterior_layer_gain)[None, :]
        meansq = lax.optimization_barrier(jnp.mean(summed * summed, axis=1, keepdims=True))
        hidden = (summed * lax.rsqrt(meansq + 1e-06) * (1.0 + closing_layer_gain)[None, :]).astype(jnp.bfloat16)
        lexicon_logit_matrix = lax.dot_general(hidden, lexicon_matrix, (((1,), (1,)), ((), ())), preferred_element_type=jnp.float32)
        valid = slot_ids[None, :] < prohibited_segment_total[generation_position][:, None]
        listed = jnp.where(valid, prohibited_segment_ids[generation_position], -1)
        block_mask = jnp.any(listed[:, :, None] == block_ids[None, None, :], axis=1)
        if generation_position == 1:
            block_mask = block_mask | ((subsequent_symbol_ids // BLOCK)[:, None] == block_ids[None, :])
        banned = jnp.repeat(block_mask, BLOCK, axis=1)
        normalized_activation = lexicon_logit_matrix / softmax_warmth[generation_position][:, None]
        masked = jnp.where(banned, -1e+30, normalized_activation)
        peak = lax.optimization_barrier(jnp.max(masked, axis=1, keepdims=True))
        total = lax.optimization_barrier(jnp.sum(jnp.where(banned, 0.0, jnp.exp(masked - peak)), axis=1, keepdims=True))
        lse = peak + jnp.log(total)
        results.append(jnp.where(banned, -30.0, normalized_activation - lse))
    return jnp.stack(results)
```

```python
import functools

import jax
import jax.numpy as jnp
from jax import lax
from jax.experimental import pallas as pl
from jax.experimental.pallas import tpu as pltpu
from jax.sharding import PartitionSpec as P

BLOCK = 2048
NB = 16
ROWS = 128
D = 5376
COLS = 168
CHUNK = 24
PART = 176
CHIP = 336
VOC = 1024
HALF = D // 2
MESH = pl.DeviceIdType.MESH
F32, BF16 = jnp.float32, jnp.bfloat16
EPS = 1e-6


def place(z, x, y, c):
    return (z, (x * 4 + y) * 2 + c)


def split16(s):
    hi = s.astype(BF16).astype(F32)
    return hi, (s - hi)


def column(value):
    n = value.shape[0]
    wide = jnp.concatenate([value, jnp.zeros((n, 256 - COLS), F32)], axis=1)
    return wide.T[: 8 * CHUNK]


def kernel(
    a_hbm, w_hbm, g1_hbm, skip_hbm, g2_hbm, l_hbm, warm_hbm, ids_hbm, tot_hbm, sub_hbm,
    scaled_hbm, shift_hbm,
    a_v, w_v, g1_v, skip_v, g2_v, l_v, warm_v, ids_v, tot_v, sub_v,
    p_t, skip_t, g1_t, g2_t, rs, zb, ub, vb, nat, uacc, vacc, out_v, shift_v, la, lb, info, stat,
    in_sem, l_sem, rs_s, rs_r, zb_s, zb_r, u_s, u_r, v_s, v_r, uf_s, uf_r, vf_s, vf_r,
    la_s, la_r, lb_s, lb_r, out_sem,
):
    z = lax.axis_index("tensor")
    v = lax.axis_index("vocab")
    x, y, c = v // 8, (v // 2) % 4, v % 2
    chip = x * 4 + y
    other = 1 - c

    def copy_in(src, dst, sem):
        d = pltpu.make_async_copy(src, dst, sem)
        d.start()
        return d

    def remote(src, dst, s, r, to):
        return pltpu.make_async_remote_copy(src, dst, s, r, device_id=to, device_id_type=MESH)

    pairs = [
        (a_hbm, a_v), (w_hbm, w_v), (skip_hbm, skip_v), (g1_hbm, g1_v), (g2_hbm, g2_v),
        (warm_hbm, warm_v), (ids_hbm, ids_v), (tot_hbm, tot_v), (sub_hbm, sub_v),
    ]
    ins = [copy_in(s, d, in_sem.at[i]) for i, (s, d) in enumerate(pairs)]
    l_in = [
        copy_in(l_hbm.at[pl.ds(i * 256, 256)], l_v.at[pl.ds(i * 256, 256)], l_sem.at[i])
        for i in range(4)
    ]

    zpeer = [place((z + k) % 8, x, y, c) for k in range(8)]
    plane = [place(z, (x + k // 4) % 4, (y + k % 4) % 4, c) for k in range(16)]
    plane_from = [((x + 4 - k // 4) % 4) * 4 + (y + 4 - k % 4) % 4 for k in range(16)]
    zboth = [place((z + k // 2) % 8, x, y, (c + k % 2) % 2) for k in range(16)]
    sibling = place(z, x, y, other)

    barrier = pltpu.get_barrier_semaphore()
    for peer in plane[1:] + zboth[1:]:
        pl.semaphore_signal(barrier, inc=1, device_id=peer, device_id_type=MESH)

    for i in (2, 3, 4):
        ins[i].wait()
    skip_t[...] = column(skip_v[...].astype(F32))
    g1_t[...] = column(1.0 + jnp.broadcast_to(g1_v[...], (ROWS, COLS)))
    g2_t[...] = column(1.0 + jnp.broadcast_to(g2_v[...], (ROWS, COLS)))

    def framed(body, extra):
        low = jnp.concatenate([body, extra], axis=0)
        high = jnp.concatenate([extra, body], axis=0)
        return jnp.where(c == 0, low, high).astype(BF16)

    vb[chip, c] = framed(skip_t[:COLS] * g2_t[:COLS], jnp.zeros((8, ROWS), F32))
    pl.semaphore_wait(barrier, 30)

    def spread(buf, s, r, f_s, f_r):
        own = buf.at[chip, c]
        sends = [remote(own, own, s.at[k], r.at[k], plane[k]) for k in range(1, 16)]
        for d in sends:
            d.start()
        forwards = [remote(own, own, f_s.at[0], f_r.at[0], sibling)]
        forwards[0].start()
        return sends, forwards

    def forward(buf, sends, forwards, k, f_s, f_r):
        sends[k - 1].wait_recv()
        got = buf.at[plane_from[k], c]
        d = remote(got, got, f_s.at[k], f_r.at[k], sibling)
        d.start()
        forwards.append(d)

    v_sends, v_forwards = spread(vb, v_s, v_r, vf_s, vf_r)

    ins[0].wait()
    ins[1].wait()
    p_t[:COLS] = lax.dot_general(
        w_v[...], a_v[...], (((1,), (1,)), ((), ())), preferred_element_type=F32
    )
    p_t[COLS:] = jnp.zeros((8 * CHUNK - COLS, ROWS), F32)
    rs_sends = []
    for k in range(1, 8):
        to = (z + k) % 8
        d = remote(
            p_t.at[pl.ds(pl.multiple_of(to * CHUNK, 8), CHUNK)], rs.at[k], rs_s.at[k], rs_r.at[k],
            zpeer[k],
        )
        d.start()
        rs_sends.append(d)

    for i in (5, 6, 7, 8):
        ins[i].wait()
    block = (z * 32 + v) * VOC // BLOCK
    slot = lax.broadcasted_iota(jnp.int32, (NB, 64), 0)
    listed = []
    for s in range(2):
        hit = (ids_v[s] == block) & (slot < tot_v[s : s + 1])
        listed.append(jnp.max(jnp.where(hit, 1.0, 0.0), axis=0, keepdims=True))
    banned = jnp.concatenate(listed, axis=1)
    fed = jnp.where((sub_v[...] >> 11) == block, 1.0, 0.0)
    fed = jnp.concatenate([jnp.zeros((1, 64), F32), fed], axis=1)
    info[0:1] = jnp.maximum(banned, fed)
    warm = warm_v[...]
    info[1:2] = 1.0 / jnp.concatenate([warm[0:1], warm[1:2]], axis=1)

    mine = pl.ds(pl.multiple_of(z * CHUNK, 8), CHUNK)
    p = p_t[mine]
    for k in range(1, 8):
        rs_sends[k - 1].wait_recv()
        p = p + rs[k]
    gained = p * g1_t[mine]
    skip = skip_t[mine]
    stats = [
        jnp.sum(t, axis=0, keepdims=True) for t in (p * p, skip * skip, skip * gained, gained * gained)
    ]
    stats = jnp.concatenate(stats, axis=0)
    hi, lo = split16(stats)
    zb[z] = jnp.concatenate([gained * g2_t[mine], hi, lo], axis=0).astype(BF16)
    zb_sends = []
    for k in range(1, 8):
        d = remote(zb.at[z], zb.at[z], zb_s.at[k], zb_r.at[k], zpeer[k])
        d.start()
        zb_sends.append(d)

    for k in range(1, 16):
        forward(vb, v_sends, v_forwards, k, vf_s, vf_r)

    for d in zb_sends:
        d.wait_recv()
    parts = [zb[i].astype(F32) for i in range(7)]
    total = sum(q[CHUNK:] for q in parts)
    total = total[:4] + total[4:]
    hi, lo = split16(total)
    ub[chip, c] = framed(
        jnp.concatenate([q[:CHUNK] for q in parts], axis=0), jnp.concatenate([hi, lo], axis=0)
    )
    u_sends, u_forwards = spread(ub, u_s, u_r, uf_s, uf_r)

    def merge(buf, i):
        base = i * CHIP
        nat[pl.ds(pl.multiple_of(base, 16), 160)] = buf[i, 0, 0:160]
        e0 = buf[i, 0, 160:176].astype(F32)
        e1 = buf[i, 1, 0:16].astype(F32)
        edge = jnp.concatenate([e0[:8], e1[8:]], axis=0)
        nat[pl.ds(pl.multiple_of(base + 160, 16), 16)] = edge.astype(BF16)
        nat[pl.ds(pl.multiple_of(base + 176, 16), 160)] = buf[i, 1, 16:176]
        return e0[8:] + e1[:8]

    def product(acc, half, first):
        cols = pl.ds(pl.multiple_of(half * HALF, 128), HALF)
        for m in range(4):
            rows = pl.ds(m * 256, 256)
            t = jnp.dot(l_v[rows, cols], nat[cols], preferred_element_type=F32)
            acc[rows] = t if first else acc[rows] + t

    for d in v_forwards:
        d.wait_recv()
    for i in range(16):
        merge(vb, i)
    for d in l_in:
        d.wait()
    product(vacc, 0, True)
    product(vacc, 1, False)

    for k in range(1, 16):
        forward(ub, u_sends, u_forwards, k, uf_s, uf_r)
    for d in u_forwards:
        d.wait_recv()
    total = merge(ub, 0)
    for i in range(1, 16):
        total = total + merge(ub, i)
    stat[...] = total
    product(uacc, 0, True)
    product(uacc, 1, False)

    total = stat[:4] + stat[4:]
    r1 = lax.rsqrt(total[0:1] / D + EPS)
    square = total[1:2] + 2.0 * r1 * total[2:3] + r1 * r1 * total[3:4]
    r2 = lax.rsqrt(jnp.maximum(square, 0.0) / D + EPS)
    warmth = r2 * info[1:2]
    banned = info[0:1]
    peak = jnp.full((1, ROWS), -jnp.inf, F32)
    for m in range(4):
        rows = pl.ds(m * 256, 256)
        t = (vacc[rows] + r1 * uacc[rows]) * warmth
        vacc[rows] = t
        peak = jnp.maximum(peak, jnp.max(t, axis=0, keepdims=True))
    mass = jnp.zeros((1, ROWS), F32)
    for m in range(4):
        mass = mass + jnp.sum(jnp.exp(vacc[pl.ds(m * 256, 256)] - peak), axis=0, keepdims=True)
    lse = jnp.where(banned > 0.0, -1e30, peak + jnp.log(mass))

    def combine(buf, s, r, peers, lse):
        buf[0] = lse
        sends = [remote(buf.at[0], buf.at[k], s.at[k], r.at[k], peers[k]) for k in range(1, 16)]
        for d in sends:
            d.start()
        return sends

    def combined(buf, sends):
        for d in sends:
            d.wait_recv()
        values = [buf[k] for k in range(16)]
        top = functools.reduce(jnp.maximum, values)
        return top + jnp.log(sum(jnp.exp(q - top) for q in values))

    la_sends = combine(la, la_s, la_r, plane, lse)
    for m in range(8):
        t = vacc[pl.ds(m * 128, 128)]
        out_v[:, pl.ds(m * 128, 128)] = jnp.where(banned > 0.0, -30.0, t).T
    out_copy = copy_in(out_v, scaled_hbm, out_sem.at[0])
    lse = combined(la, la_sends)
    lb_sends = combine(lb, lb_s, lb_r, zboth, lse)
    lse = combined(lb, lb_sends)
    shift_v[...] = jnp.broadcast_to(jnp.where(banned > 0.0, 0.0, lse), (ROWS, ROWS)).T
    shift_copy = copy_in(shift_v, shift_hbm, out_sem.at[1])

    for group in (v_sends, v_forwards, rs_sends, zb_sends, u_sends, u_forwards, la_sends, lb_sends):
        for d in group:
            d.wait_send()
    out_copy.wait()
    shift_copy.wait()


def local(a, w, g1, skip, g2, lexicon, warm, ids, total, sub):
    dma = pltpu.SemaphoreType.DMA
    vm = pltpu.VMEM
    scaled, shift = pl.pallas_call(
        kernel,
        name="head",
        out_shape=(
            jax.ShapeDtypeStruct((ROWS, VOC), F32),
            jax.ShapeDtypeStruct((ROWS, ROWS), F32),
        ),
        in_specs=[pl.BlockSpec(memory_space=pl.ANY)] * 10,
        out_specs=(pl.BlockSpec(memory_space=pl.ANY),) * 2,
        scratch_shapes=[
            vm((ROWS, 2688), BF16),
            vm((COLS, 2688), BF16),
            vm((1, COLS), F32),
            vm((ROWS, COLS), BF16),
            vm((1, COLS), F32),
            vm((VOC, D), BF16),
            vm((2, 64), F32),
            vm((2, NB, 64), jnp.int32),
            vm((2, 64), jnp.int32),
            vm((1, 64), jnp.int32),
            vm((8 * CHUNK, ROWS), F32),
            vm((8 * CHUNK, ROWS), F32),
            vm((8 * CHUNK, ROWS), F32),
            vm((8 * CHUNK, ROWS), F32),
            vm((8, CHUNK, ROWS), F32),
            vm((8, 32, ROWS), BF16),
            vm((16, 2, PART, ROWS), BF16),
            vm((16, 2, PART, ROWS), BF16),
            vm((D, ROWS), BF16),
            vm((VOC, ROWS), F32),
            vm((VOC, ROWS), F32),
            vm((ROWS, VOC), F32),
            vm((ROWS, ROWS), F32),
            vm((16, 1, ROWS), F32),
            vm((16, 1, ROWS), F32),
            vm((8, ROWS), F32),
            vm((8, ROWS), F32),
            dma((9,)),
            dma((4,)),
        ]
        + [dma((8,))] * 4
        + [dma((16,))] * 12
        + [dma((2,))],
        compiler_params=pltpu.CompilerParams(
            collective_id=0, has_side_effects=True, vmem_limit_bytes=63 * 1024 * 1024
        ),
    )(
        a.reshape(ROWS, 2688),
        w.T,
        g1.reshape(1, COLS),
        skip.reshape(ROWS, COLS),
        g2.reshape(1, COLS),
        lexicon,
        warm,
        ids.transpose(0, 2, 1),
        total,
        sub.reshape(1, 64),
    )
    return (scaled - shift[:, :1]).reshape(2, 64, VOC)


def solution(mesh):
    placed = (
        P(None, None, "tensor"),
        P("tensor", "vocab"),
        P("vocab"),
        P(None, None, "vocab"),
        P("vocab"),
        P(("tensor", "vocab"), None),
        P(),
        P(),
        P(),
        P(),
    )
    return jax.shard_map(
        local,
        mesh=mesh,
        in_specs=placed,
        out_specs=P(None, None, ("tensor", "vocab")),
        check_vma=False,
    )
```

```python
import functools

import jax
import jax.numpy as jnp
from jax import lax
from jax.experimental import pallas as pl
from jax.experimental.pallas import tpu as pltpu
from jax.sharding import PartitionSpec as P

BLOCK = 2048
NB = 16
ROWS = 128
D = 5376
COLS = 168
CHUNK = 24
PART = 176
CHIP = 336
VOC = 1024
HALF = D // 2
MESH = pl.DeviceIdType.MESH
ZLINE = (4, 3, 5, 2, 6, 1, 7, 0)
ZBOTH = (8, 9, 6, 7, 10, 11, 4, 5, 12, 13, 2, 3, 14, 15, 1)
PLANE = (10, 2, 8, 11, 9, 6, 14, 3, 1, 4, 12, 5, 7, 13, 15)
F32, BF16 = jnp.float32, jnp.bfloat16
EPS = 1e-6


def place(z, x, y, c):
    return (z, (x * 4 + y) * 2 + c)


def split16(s):
    hi = s.astype(BF16).astype(F32)
    return hi, (s - hi)


def column(value):
    n = value.shape[0]
    wide = jnp.concatenate([value, jnp.zeros((n, 256 - COLS), F32)], axis=1)
    return wide.T[:COLS]


def kernel(
    a_hbm, w_hbm, g1_hbm, skip_hbm, g2_hbm, l_hbm, warm_hbm, ids_hbm, tot_hbm, sub_hbm,
    scaled_hbm, shift_hbm,
    a_v, w_v, g1_v, skip_v, g2_v, l_v, warm_v, ids_v, tot_v, sub_v,
    skip_t, g1_t, g2_t, part, rs, sums, zb, ub, vb, nat, uacc, vacc, out_v, shift_v, la, lb, info, stat,
    in_sem, l_sem, rs_s, rs_r, zb_s, zb_r, u_s, u_r, v_s, v_r, uf_s, uf_r, vf_s, vf_r,
    la_s, la_r, lb_s, lb_r, out_sem,
):
    z = lax.axis_index("tensor")
    v = lax.axis_index("vocab")
    x, y, c = v // 8, (v // 2) % 4, v % 2
    chip = x * 4 + y
    other = 1 - c

    def copy_in(src, dst, sem):
        d = pltpu.make_async_copy(src, dst, sem)
        d.start()
        return d

    def remote(src, dst, s, r, to):
        return pltpu.make_async_remote_copy(src, dst, s, r, device_id=to, device_id_type=MESH)

    pairs = [
        (a_hbm, a_v), (w_hbm, w_v), (skip_hbm, skip_v), (g1_hbm, g1_v), (g2_hbm, g2_v),
        (warm_hbm, warm_v), (ids_hbm, ids_v), (tot_hbm, tot_v), (sub_hbm, sub_v),
    ]
    zline = [place((z + k) % 8, x, y, other) for k in range(8)]
    plane = [place(z, x ^ (k // 4), y ^ (k % 4), other) for k in range(16)]
    plane_from = [(x ^ (k // 4)) * 4 + (y ^ (k % 4)) for k in range(16)]
    zboth = [place((z + k // 2) % 8, x, y, (c + k % 2) % 2) for k in range(16)]
    sibling = plane[0]

    ins = [copy_in(s, d, in_sem.at[i]) for i, (s, d) in enumerate(pairs[:2])]
    barrier = pltpu.get_barrier_semaphore()
    for peer in [zboth[k] for k in ZBOTH] + [plane[k] for k in PLANE]:
        pl.semaphore_signal(barrier, inc=1, device_id=peer, device_id_type=MESH)
    ins += [copy_in(s, d, in_sem.at[i + 2]) for i, (s, d) in enumerate(pairs[2:])]
    l_in = [
        copy_in(l_hbm.at[pl.ds(i * 256, 256)], l_v.at[pl.ds(i * 256, 256)], l_sem.at[i])
        for i in range(4)
    ]

    def framed(body, extra, core):
        low = jnp.concatenate([body, extra], axis=0)
        high = jnp.concatenate([extra, body], axis=0)
        return jnp.where(core == 0, low, high).astype(BF16)

    def spread(buf, core, s, r, f_s, f_r):
        own = buf.at[chip, core]
        forwards = [remote(own, own, f_s.at[0], f_r.at[0], sibling)]
        sends = [remote(own, own, s.at[k], r.at[k], plane[k]) for k in range(1, 16)]
        for d in sends + forwards:
            d.start()
        return sends, forwards

    def forward(buf, core, sends, forwards, quarter, f_s, f_r):
        for k in range(max(1, quarter * 4), quarter * 4 + 4):
            sends[k - 1].wait_recv()
            got = buf.at[plane_from[k], 1 - core]
            d = remote(got, got, f_s.at[k], f_r.at[k], sibling)
            d.start()
            forwards.append(d)

    def merge(buf, pair):
        half = (x // 2) ^ pair
        forwards = v_forwards if buf is vb else u_forwards
        for d in forwards[pair * 8 : pair * 8 + 8]:
            d.wait_recv()
        total = jnp.zeros((8, ROWS), F32)
        for j in range(8):
            base = j * CHIP
            got = buf.at[half * 8 + j]
            nat[base : base + 160] = got[0, 0:160]
            e0 = got[0, 160:176].astype(F32)
            e1 = got[1, 0:16].astype(F32)
            edge = jnp.concatenate([e0[:8], e1[8:]], axis=0)
            nat[base + 160 : base + 176] = edge.astype(BF16)
            nat[base + 176 : base + 336] = got[1, 16:176]
            total = total + (e0[8:] + e1[:8])
        return total

    def product(acc, pair, tiles):
        cols = pl.ds(pl.multiple_of(((x // 2) ^ pair) * HALF, 128), HALF)
        for m in tiles:
            rows = pl.ds(m * 256, 256)
            t = jnp.dot(l_v[rows, cols], nat[...], preferred_element_type=F32)
            acc[rows] = t if pair == 0 else acc[rows] + t

    ins[0].wait()
    ins[1].wait()
    part[:COLS] = lax.dot_general(
        w_v[...], a_v[...], (((1,), (1,)), ((), ())), preferred_element_type=F32
    )
    part[COLS:] = jnp.zeros((8 * CHUNK - COLS, ROWS), F32)
    pl.semaphore_wait(barrier, 30)
    rs_sends = {}
    for k in ZLINE:
        chunk = part.at[pl.ds(pl.multiple_of((z + k) % 8 * CHUNK, 8), CHUNK)]
        rs_sends[k] = remote(chunk, rs.at[k], rs_s.at[k], rs_r.at[k], zline[k])
        rs_sends[k].start()

    for i in (2, 3, 4):
        ins[i].wait()
    skip_t[...] = column(skip_v[...].astype(F32))
    g1_t[...] = column(1.0 + jnp.broadcast_to(g1_v[...], (ROWS, COLS)))
    g2_t[...] = column(1.0 + jnp.broadcast_to(g2_v[...], (ROWS, COLS)))
    vb[chip, c] = framed(skip_t[...] * g2_t[...], jnp.zeros((8, ROWS), F32), c)
    v_sends, v_forwards = spread(vb, c, v_s, v_r, vf_s, vf_r)

    for i in (5, 6, 7, 8):
        ins[i].wait()
    block = (z * 32 + v) * VOC // BLOCK
    slot = lax.broadcasted_iota(jnp.int32, (NB, 64), 0)
    listed = []
    for s in range(2):
        hit = (ids_v[s] == block) & (slot < tot_v[s : s + 1])
        listed.append(jnp.max(jnp.where(hit, 1.0, 0.0), axis=0, keepdims=True))
    banned = jnp.concatenate(listed, axis=1)
    fed = jnp.where((sub_v[...] >> 11) == block, 1.0, 0.0)
    fed = jnp.concatenate([jnp.zeros((1, 64), F32), fed], axis=1)
    info[0:1] = jnp.maximum(banned, fed)
    warm = warm_v[...]
    info[1:2] = 1.0 / jnp.concatenate([warm[0:1], warm[1:2]], axis=1)

    total = jnp.zeros((CHUNK, ROWS), F32)
    for k in reversed(ZLINE):
        rs_sends[k].wait_recv()
        total = total + rs[k]
    sums[...] = total
    zb_sends = []
    for k in ZLINE:
        chunk = zb.at[pl.ds(pl.multiple_of(z * CHUNK, 8), CHUNK)]
        zb_sends.append(remote(sums, chunk, zb_s.at[k], zb_r.at[k], zline[k]))
        zb_sends[-1].start()
    for d in reversed(zb_sends):
        d.wait_recv()
    p = zb[:COLS]
    skip = skip_t[...]
    gained = p * g1_t[...]
    stats = [
        jnp.sum(t, axis=0, keepdims=True) for t in (p * p, skip * skip, skip * gained, gained * gained)
    ]
    hi, lo = split16(jnp.concatenate(stats, axis=0))
    ub[chip, c] = framed(gained * g2_t[...], jnp.concatenate([hi, lo], axis=0), c)
    u_sends, u_forwards = spread(ub, c, u_s, u_r, uf_s, uf_r)

    forward(vb, c, v_sends, v_forwards, 0, vf_s, vf_r)
    forward(vb, c, v_sends, v_forwards, 1, vf_s, vf_r)
    forward(vb, c, v_sends, v_forwards, 2, vf_s, vf_r)
    forward(vb, c, v_sends, v_forwards, 3, vf_s, vf_r)
    for d in l_in:
        d.wait()
    for pair in range(2):
        merge(vb, pair)
        product(vacc, pair, range(4))
    forward(ub, c, u_sends, u_forwards, 0, uf_s, uf_r)
    forward(ub, c, u_sends, u_forwards, 1, uf_s, uf_r)
    stat[...] = merge(ub, 0)
    product(uacc, 0, (0, 1))
    forward(ub, c, u_sends, u_forwards, 2, uf_s, uf_r)
    forward(ub, c, u_sends, u_forwards, 3, uf_s, uf_r)
    product(uacc, 0, (2, 3))
    stat[...] += merge(ub, 1)
    product(uacc, 1, range(4))

    total = stat[:4] + stat[4:]
    r1 = lax.rsqrt(total[0:1] / D + EPS)
    square = total[1:2] + 2.0 * r1 * total[2:3] + r1 * r1 * total[3:4]
    r2 = lax.rsqrt(jnp.maximum(square, 0.0) / D + EPS)
    warmth = r2 * info[1:2]
    banned = info[0:1]
    peak = jnp.full((1, ROWS), -jnp.inf, F32)
    for m in range(4):
        rows = pl.ds(m * 256, 256)
        t = (vacc[rows] + r1 * uacc[rows]) * warmth
        vacc[rows] = t
        peak = jnp.maximum(peak, jnp.max(t, axis=0, keepdims=True))
    mass = jnp.zeros((1, ROWS), F32)
    for m in range(4):
        mass = mass + jnp.sum(jnp.exp(vacc[pl.ds(m * 256, 256)] - peak), axis=0, keepdims=True)
    lse = jnp.where(banned > 0.0, -1e30, peak + jnp.log(mass))

    def sent(*groups):
        for group in groups:
            for d in group:
                d.wait_send()

    def combine(mine, buf, s, r, peers, order, lse):
        mine[...] = lse
        sends = [remote(mine, buf.at[k], s.at[k], r.at[k], peers[k]) for k in order]
        for d in sends:
            d.start()
        return sends

    def combined(buf, sends):
        for d in sends:
            d.wait_recv()
        values = [buf[k] for k in range(16)]
        top = functools.reduce(jnp.maximum, values)
        return top + jnp.log(sum(jnp.exp(q - top) for q in values))

    la_sends = combine(la.at[16], la, la_s, la_r, plane, PLANE + (0,), lse)
    for m in range(8):
        t = vacc[pl.ds(m * 128, 128)]
        out_v[:, pl.ds(m * 128, 128)] = jnp.where(banned > 0.0, -30.0, t).T
    out_copy = copy_in(out_v, scaled_hbm, out_sem.at[0])
    sent(v_sends, v_forwards, rs_sends.values(), zb_sends)
    lse = combined(la, la_sends)
    lb_sends = combine(lb.at[0], lb, lb_s, lb_r, zboth, ZBOTH, lse)
    sent(u_sends, u_forwards, la_sends)
    lse = combined(lb, lb_sends)
    shift_v[...] = jnp.where(banned > 0.0, 0.0, lse)
    shift_copy = copy_in(shift_v, shift_hbm, out_sem.at[1])
    sent(lb_sends)
    out_copy.wait()
    shift_copy.wait()


def local(a, w, g1, skip, g2, lexicon, warm, ids, total, sub):
    dma = pltpu.SemaphoreType.DMA
    vm = pltpu.VMEM
    scaled, shift = pl.pallas_call(
        kernel,
        name="head",
        out_shape=(
            jax.ShapeDtypeStruct((ROWS, VOC), F32),
            jax.ShapeDtypeStruct((1, ROWS), F32),
        ),
        in_specs=[pl.BlockSpec(memory_space=pl.ANY)] * 10,
        out_specs=(pl.BlockSpec(memory_space=pl.ANY),) * 2,
        scratch_shapes=[
            vm((ROWS, 2688), BF16),
            vm((COLS, 2688), BF16),
            vm((1, COLS), F32),
            vm((ROWS, COLS), BF16),
            vm((1, COLS), F32),
            vm((VOC, D), BF16),
            vm((2, 64), F32),
            vm((2, NB, 64), jnp.int32),
            vm((2, 64), jnp.int32),
            vm((1, 64), jnp.int32),
        ]
        + [vm((COLS, ROWS), F32)] * 3
        + [
            vm((8 * CHUNK, ROWS), F32),
            vm((8, CHUNK, ROWS), F32),
            vm((CHUNK, ROWS), F32),
            vm((8 * CHUNK, ROWS), F32),
            vm((16, 2, PART, ROWS), BF16),
            vm((16, 2, PART, ROWS), BF16),
            vm((HALF, ROWS), BF16),
            vm((VOC, ROWS), F32),
            vm((VOC, ROWS), F32),
            vm((ROWS, VOC), F32),
            vm((1, ROWS), F32),
            vm((17, 1, ROWS), F32),
            vm((16, 1, ROWS), F32),
            vm((8, ROWS), F32),
            vm((8, ROWS), F32),
            dma((9,)),
            dma((4,)),
        ]
        + [dma((8,))] * 4
        + [dma((16,))] * 12
        + [dma((2,))],
        compiler_params=pltpu.CompilerParams(
            collective_id=0, has_side_effects=True, vmem_limit_bytes=63 * 1024 * 1024
        ),
    )(
        a.reshape(ROWS, 2688),
        w.T,
        g1.reshape(1, COLS),
        skip.reshape(ROWS, COLS),
        g2.reshape(1, COLS),
        lexicon,
        warm,
        ids.transpose(0, 2, 1),
        total,
        sub.reshape(1, 64),
    )
    return (scaled - shift.reshape(ROWS, 1)).reshape(2, 64, VOC)


def solution(mesh):
    placed = (
        P(None, None, "tensor"),
        P("tensor", "vocab"),
        P("vocab"),
        P(None, None, "vocab"),
        P("vocab"),
        P(("tensor", "vocab"), None),
        P(),
        P(),
        P(),
        P(),
    )
    return jax.shard_map(
        local,
        mesh=mesh,
        in_specs=placed,
        out_specs=P(None, None, ("tensor", "vocab")),
        check_vma=False,
    )
```

```python
import functools

import jax
import jax.numpy as jnp
from jax import lax
from jax.experimental import pallas as pl
from jax.experimental.pallas import tpu as pltpu
from jax.sharding import PartitionSpec as P

BLOCK = 2048
NB = 16
ROWS = 128
D = 5376
COLS = 168
CHUNK = 24
PART = 176
CHIP = 336
VOC = 1024
HALF = D // 2
MESH = pl.DeviceIdType.MESH
ZLINE = (4, 3, 5, 2, 6, 1, 7, 0)
ZBOTH = (8, 9, 6, 7, 10, 11, 4, 5, 12, 13, 2, 3, 14, 15, 1)
SPREAD = (10, 11, 9, 6, 14, 2, 8, 5, 7, 13, 15, 1, 3, 4, 12)
FIRST = 0
PLANE = (10, 11, 9, 6, 14, 2, 8, 5, 7, 13, 15, 1, 3, 4, 12)
F32, BF16 = jnp.float32, jnp.bfloat16
EPS = 1e-6


def place(z, x, y, c):
    return (z, (x * 4 + y) * 2 + c)


def split16(s):
    hi = s.astype(BF16).astype(F32)
    return hi, (s - hi)


def column(value):
    n = value.shape[0]
    wide = jnp.concatenate([value, jnp.zeros((n, 256 - COLS), F32)], axis=1)
    return wide.T[:COLS]


def kernel(
    a_hbm, w_hbm, g1_hbm, skip_hbm, g2_hbm, l_hbm, warm_hbm, ids_hbm, tot_hbm, sub_hbm,
    scaled_hbm, shift_hbm,
    a_v, w_v, g1_v, skip_v, g2_v, l_v, warm_v, ids_v, tot_v, sub_v,
    skip_t, g1_t, g2_t, part, rs, sums, zb, ub, vb, nat, uacc, vacc, out_v, shift_v, la, lb, info, stat,
    in_sem, l_sem, rs_s, rs_r, zb_s, zb_r, u_s, u_r, v_s, v_r, uf_s, uf_r, vf_s, vf_r,
    la_s, la_r, lb_s, lb_r, out_sem,
):
    z = lax.axis_index("tensor")
    v = lax.axis_index("vocab")
    x, y, c = v // 8, (v // 2) % 4, v % 2
    chip = x * 4 + y
    other = 1 - c

    def copy_in(src, dst, sem):
        d = pltpu.make_async_copy(src, dst, sem)
        d.start()
        return d

    def remote(src, dst, s, r, to):
        return pltpu.make_async_remote_copy(src, dst, s, r, device_id=to, device_id_type=MESH)

    pairs = [
        (a_hbm, a_v), (w_hbm, w_v), (skip_hbm, skip_v), (g1_hbm, g1_v), (g2_hbm, g2_v),
        (warm_hbm, warm_v), (ids_hbm, ids_v), (tot_hbm, tot_v), (sub_hbm, sub_v),
    ]
    zline = [place((z + k) % 8, x, y, other) for k in range(8)]
    plane = [place(z, x ^ (k // 4), y ^ (k % 4), other) for k in range(16)]
    plane_from = [(x ^ (k // 4)) * 4 + (y ^ (k % 4)) for k in range(16)]
    zboth = [place((z + k // 2) % 8, x, y, (c + k % 2) % 2) for k in range(16)]
    sibling = plane[0]

    ins = [copy_in(s, d, in_sem.at[i]) for i, (s, d) in enumerate(pairs[:2])]
    barrier = pltpu.get_barrier_semaphore()
    for peer in [zboth[k] for k in ZBOTH] + [plane[k] for k in PLANE]:
        pl.semaphore_signal(barrier, inc=1, device_id=peer, device_id_type=MESH)
    ins += [copy_in(s, d, in_sem.at[i + 2]) for i, (s, d) in enumerate(pairs[2:])]
    l_in = [
        copy_in(l_hbm.at[pl.ds(i * 256, 256)], l_v.at[pl.ds(i * 256, 256)], l_sem.at[i])
        for i in range(4)
    ]

    def framed(body, extra, core):
        low = jnp.concatenate([body, extra], axis=0)
        high = jnp.concatenate([extra, body], axis=0)
        return jnp.where(core == 0, low, high).astype(BF16)

    def spread(buf, core, s, r, f_s, f_r):
        own = buf.at[chip, core]
        forwards = {0: remote(own, own, f_s.at[0], f_r.at[0], sibling)}
        sends = {k: remote(own, own, s.at[k], r.at[k], plane[k]) for k in SPREAD}
        for d in [*sends.values(), forwards[0]]:
            d.start()
        return sends, forwards

    def forward(buf, core, sends, forwards, order, f_s, f_r):
        for k in order:
            sends[k].wait_recv()
            got = buf.at[plane_from[k], 1 - core]
            forwards[k] = remote(got, got, f_s.at[k], f_r.at[k], sibling)
            forwards[k].start()

    def merge(buf, pair):
        half = (x // 2) ^ pair
        forwards = v_forwards if buf is vb else u_forwards
        for k in range(pair * 8, pair * 8 + 8):
            forwards[k].wait_recv()
        total = jnp.zeros((8, ROWS), F32)
        for j in range(8):
            base = j * CHIP
            got = buf.at[half * 8 + j]
            nat[base : base + 160] = got[0, 0:160]
            e0 = got[0, 160:176].astype(F32)
            e1 = got[1, 0:16].astype(F32)
            edge = jnp.concatenate([e0[:8], e1[8:]], axis=0)
            nat[base + 160 : base + 176] = edge.astype(BF16)
            nat[base + 176 : base + 336] = got[1, 16:176]
            total = total + (e0[8:] + e1[:8])
        return total

    def product(acc, pair, tiles):
        cols = pl.ds(pl.multiple_of(((x // 2) ^ pair) * HALF, 128), HALF)
        for m in tiles:
            rows = pl.ds(m * 256, 256)
            t = jnp.dot(l_v[rows, cols], nat[...], preferred_element_type=F32)
            acc[rows] = t if pair == FIRST else acc[rows] + t

    ins[0].wait()
    ins[1].wait()
    part[:COLS] = lax.dot_general(
        w_v[...], a_v[...], (((1,), (1,)), ((), ())), preferred_element_type=F32
    )
    part[COLS:] = jnp.zeros((8 * CHUNK - COLS, ROWS), F32)
    pl.semaphore_wait(barrier, 30)
    rs_sends = {}
    for k in ZLINE:
        chunk = part.at[pl.ds(pl.multiple_of((z + k) % 8 * CHUNK, 8), CHUNK)]
        rs_sends[k] = remote(chunk, rs.at[k], rs_s.at[k], rs_r.at[k], zline[k])
        rs_sends[k].start()

    for i in (2, 3, 4):
        ins[i].wait()
    skip_t[...] = column(skip_v[...].astype(F32))
    g1_t[...] = column(1.0 + jnp.broadcast_to(g1_v[...], (ROWS, COLS)))
    g2_t[...] = column(1.0 + jnp.broadcast_to(g2_v[...], (ROWS, COLS)))
    vb[chip, c] = framed(skip_t[...] * g2_t[...], jnp.zeros((8, ROWS), F32), c)
    v_sends, v_forwards = spread(vb, c, v_s, v_r, vf_s, vf_r)

    for i in (5, 6, 7, 8):
        ins[i].wait()
    block = (z * 32 + v) * VOC // BLOCK
    slot = lax.broadcasted_iota(jnp.int32, (NB, 64), 0)
    listed = []
    for s in range(2):
        hit = (ids_v[s] == block) & (slot < tot_v[s : s + 1])
        listed.append(jnp.max(jnp.where(hit, 1.0, 0.0), axis=0, keepdims=True))
    banned = jnp.concatenate(listed, axis=1)
    fed = jnp.where((sub_v[...] >> 11) == block, 1.0, 0.0)
    fed = jnp.concatenate([jnp.zeros((1, 64), F32), fed], axis=1)
    info[0:1] = jnp.maximum(banned, fed)
    warm = warm_v[...]
    info[1:2] = 1.0 / jnp.concatenate([warm[0:1], warm[1:2]], axis=1)

    total = jnp.zeros((CHUNK, ROWS), F32)
    for k in reversed(ZLINE):
        rs_sends[k].wait_recv()
        total = total + rs[k]
    sums[...] = total
    zb_sends = []
    for k in ZLINE:
        chunk = zb.at[pl.ds(pl.multiple_of(z * CHUNK, 8), CHUNK)]
        zb_sends.append(remote(sums, chunk, zb_s.at[k], zb_r.at[k], zline[k]))
        zb_sends[-1].start()
    for d in reversed(zb_sends):
        d.wait_recv()
    p = zb[:COLS]
    skip = skip_t[...]
    gained = p * g1_t[...]
    stats = [
        jnp.sum(t, axis=0, keepdims=True) for t in (p * p, skip * skip, skip * gained, gained * gained)
    ]
    hi, lo = split16(jnp.concatenate(stats, axis=0))
    ub[chip, c] = framed(gained * g2_t[...], jnp.concatenate([hi, lo], axis=0), c)
    u_sends, u_forwards = spread(ub, c, u_s, u_r, uf_s, uf_r)

    forward(vb, c, v_sends, v_forwards, SPREAD, vf_s, vf_r)
    for d in l_in:
        d.wait()
    for pair in (FIRST, 1 - FIRST):
        merge(vb, pair)
        product(vacc, pair, range(4))
    forward(ub, c, u_sends, u_forwards, SPREAD, uf_s, uf_r)
    stat[...] = merge(ub, 0)
    product(uacc, 0, range(4))
    stat[...] += merge(ub, 1)
    total = stat[:4] + stat[4:]
    r1 = lax.rsqrt(total[0:1] / D + EPS)
    square = total[1:2] + 2.0 * r1 * total[2:3] + r1 * r1 * total[3:4]
    r2 = lax.rsqrt(jnp.maximum(square, 0.0) / D + EPS)
    warmth = r2 * info[1:2]
    banned = info[0:1]
    cols = pl.ds(pl.multiple_of((1 - x // 2) * HALF, 128), HALF)
    peaks, masses = [], []
    for m in range(4):
        rows = pl.ds(m * 256, 256)
        t = jnp.dot(l_v[rows, cols], nat[...], preferred_element_type=F32)
        t = (vacc[rows] + r1 * (uacc[rows] + t)) * warmth
        vacc[rows] = t
        peaks.append(jnp.max(t, axis=0, keepdims=True))
        masses.append(jnp.sum(jnp.exp(t - peaks[m]), axis=0, keepdims=True))
    peak = functools.reduce(jnp.maximum, peaks)
    mass = sum(w * jnp.exp(q - peak) for w, q in zip(masses, peaks))
    lse = jnp.where(banned > 0.0, -1e30, peak + jnp.log(mass))

    def sent(*groups):
        for group in groups:
            for d in group:
                d.wait_send()

    def combine(mine, buf, s, r, peers, order, lse):
        mine[...] = lse
        sends = [remote(mine, buf.at[k], s.at[k], r.at[k], peers[k]) for k in order]
        for d in sends:
            d.start()
        return sends

    def combined(buf, sends):
        for d in sends:
            d.wait_recv()
        values = [buf[k] for k in range(16)]
        top = functools.reduce(jnp.maximum, values)
        return top + jnp.log(sum(jnp.exp(q - top) for q in values))

    la_sends = combine(la.at[16], la, la_s, la_r, plane, PLANE + (0,), lse)
    for m in range(8):
        t = vacc[pl.ds(m * 128, 128)]
        out_v[:, pl.ds(m * 128, 128)] = jnp.where(banned > 0.0, -30.0, t).T
    out_copy = copy_in(out_v, scaled_hbm, out_sem.at[0])
    sent(v_sends.values(), v_forwards.values(), rs_sends.values(), zb_sends)
    lse = combined(la, la_sends)
    lb_sends = combine(lb.at[0], lb, lb_s, lb_r, zboth, ZBOTH, lse)
    sent(u_sends.values(), u_forwards.values(), la_sends)
    lse = combined(lb, lb_sends)
    shift_v[...] = jnp.where(banned > 0.0, 0.0, lse)
    shift_copy = copy_in(shift_v, shift_hbm, out_sem.at[1])
    sent(lb_sends)
    out_copy.wait()
    shift_copy.wait()


def local(a, w, g1, skip, g2, lexicon, warm, ids, total, sub):
    dma = pltpu.SemaphoreType.DMA
    vm = pltpu.VMEM
    scaled, shift = pl.pallas_call(
        kernel,
        name="head",
        out_shape=(
            jax.ShapeDtypeStruct((ROWS, VOC), F32),
            jax.ShapeDtypeStruct((1, ROWS), F32),
        ),
        in_specs=[pl.BlockSpec(memory_space=pl.ANY)] * 10,
        out_specs=(pl.BlockSpec(memory_space=pl.ANY),) * 2,
        scratch_shapes=[
            vm((ROWS, 2688), BF16),
            vm((COLS, 2688), BF16),
            vm((1, COLS), F32),
            vm((ROWS, COLS), BF16),
            vm((1, COLS), F32),
            vm((VOC, D), BF16),
            vm((2, 64), F32),
            vm((2, NB, 64), jnp.int32),
            vm((2, 64), jnp.int32),
            vm((1, 64), jnp.int32),
        ]
        + [vm((COLS, ROWS), F32)] * 3
        + [
            vm((8 * CHUNK, ROWS), F32),
            vm((8, CHUNK, ROWS), F32),
            vm((CHUNK, ROWS), F32),
            vm((8 * CHUNK, ROWS), F32),
            vm((16, 2, PART, ROWS), BF16),
            vm((16, 2, PART, ROWS), BF16),
            vm((HALF, ROWS), BF16),
            vm((VOC, ROWS), F32),
            vm((VOC, ROWS), F32),
            vm((ROWS, VOC), F32),
            vm((1, ROWS), F32),
            vm((17, 1, ROWS), F32),
            vm((16, 1, ROWS), F32),
            vm((8, ROWS), F32),
            vm((8, ROWS), F32),
            dma((9,)),
            dma((4,)),
        ]
        + [dma((8,))] * 4
        + [dma((16,))] * 12
        + [dma((2,))],
        compiler_params=pltpu.CompilerParams(
            collective_id=0, has_side_effects=True, vmem_limit_bytes=63 * 1024 * 1024
        ),
    )(
        a.reshape(ROWS, 2688),
        w.T,
        g1.reshape(1, COLS),
        skip.reshape(ROWS, COLS),
        g2.reshape(1, COLS),
        lexicon,
        warm,
        ids.transpose(0, 2, 1),
        total,
        sub.reshape(1, 64),
    )
    return (scaled - shift.reshape(ROWS, 1)).reshape(2, 64, VOC)


def solution(mesh):
    placed = (
        P(None, None, "tensor"),
        P("tensor", "vocab"),
        P("vocab"),
        P(None, None, "vocab"),
        P("vocab"),
        P(("tensor", "vocab"), None),
        P(),
        P(),
        P(),
        P(),
    )
    return jax.shard_map(
        local,
        mesh=mesh,
        in_specs=placed,
        out_specs=P(None, None, ("tensor", "vocab")),
        check_vma=False,
    )
```

```python
import functools

import jax
import jax.numpy as jnp
from jax import lax
from jax.experimental import pallas as pl
from jax.experimental.pallas import tpu as pltpu
from jax.sharding import PartitionSpec as P

BLOCK = 2048
NB = 16
ROWS = 128
D = 5376
COLS = 168
CHUNK = 24
PART = 176
CHIP = 336
VOC = 1024
HALF = D // 2
MESH = pl.DeviceIdType.MESH
ZLINE = (4, 3, 5, 2, 6, 1, 7, 0)
ZBOTH = (8, 9, 6, 7, 10, 11, 4, 5, 12, 13, 2, 3, 14, 15, 1)
SPREAD = (10, 11, 9, 6, 14, 2, 8, 5, 7, 13, 15, 1, 3, 4, 12)
FIRST = 0
PLANE = (10, 11, 9, 6, 14, 2, 8, 5, 7, 13, 15, 1, 3, 4, 12)
F32, BF16 = jnp.float32, jnp.bfloat16
EPS = 1e-6


def place(z, x, y, c):
    return (z, (x * 4 + y) * 2 + c)


def split16(s):
    hi = s.astype(BF16).astype(F32)
    return hi, (s - hi)


def column(value):
    n = value.shape[0]
    wide = jnp.concatenate([value, jnp.zeros((n, 256 - COLS), F32)], axis=1)
    return wide.T[:COLS]


def kernel(
    a_hbm, w_hbm, g1_hbm, skip_hbm, g2_hbm, l_hbm, warm_hbm, ids_hbm, tot_hbm, sub_hbm,
    scaled_hbm, shift_hbm,
    a_v, w_v, g1_v, skip_v, g2_v, l_v, warm_v, ids_v, tot_v, sub_v,
    skip_t, g1_t, g2_t, part, rs, sums, zb, ub, vb, nat, uacc, vacc, out_v, shift_v, la, lb, info, stat,
    in_sem, l_sem, rs_s, rs_r, zb_s, zb_r, u_s, u_r, v_s, v_r, uf_s, uf_r, vf_s, vf_r,
    la_s, la_r, lb_s, lb_r, out_sem,
):
    z = lax.axis_index("tensor")
    v = lax.axis_index("vocab")
    x, y, c = v // 8, (v // 2) % 4, v % 2
    chip = x * 4 + y
    other = 1 - c

    def copy_in(src, dst, sem):
        d = pltpu.make_async_copy(src, dst, sem)
        d.start()
        return d

    def remote(src, dst, s, r, to):
        return pltpu.make_async_remote_copy(src, dst, s, r, device_id=to, device_id_type=MESH)

    pairs = [
        (a_hbm, a_v), (w_hbm, w_v), (skip_hbm, skip_v), (g1_hbm, g1_v), (g2_hbm, g2_v),
        (warm_hbm, warm_v), (ids_hbm, ids_v), (tot_hbm, tot_v), (sub_hbm, sub_v),
    ]
    zline = [place((z + k) % 8, x, y, other) for k in range(8)]
    plane = [place(z, x ^ (k // 4), y ^ (k % 4), other) for k in range(16)]
    plane_from = [(x ^ (k // 4)) * 4 + (y ^ (k % 4)) for k in range(16)]
    zboth = [place((z + k // 2) % 8, x, y, (c + k % 2) % 2) for k in range(16)]
    sibling = plane[0]

    ins = [copy_in(s, d, in_sem.at[i]) for i, (s, d) in enumerate(pairs[:2])]
    barrier = pltpu.get_barrier_semaphore()
    for peer in [zboth[k] for k in ZBOTH] + [plane[k] for k in PLANE]:
        pl.semaphore_signal(barrier, inc=1, device_id=peer, device_id_type=MESH)

    @pl.when(c == 1)
    def _():
        for k in PLANE:
            to = place(z, x ^ (k // 4), y ^ (k % 4), 1)
            pl.semaphore_signal(barrier, inc=1, device_id=to, device_id_type=MESH)

    ins += [copy_in(s, d, in_sem.at[i + 2]) for i, (s, d) in enumerate(pairs[2:])]
    l_in = [
        copy_in(l_hbm.at[pl.ds(i * 256, 256)], l_v.at[pl.ds(i * 256, 256)], l_sem.at[i])
        for i in range(4)
    ]

    def framed(body, extra, core):
        low = jnp.concatenate([body, extra], axis=0)
        high = jnp.concatenate([extra, body], axis=0)
        return jnp.where(core == 0, low, high).astype(BF16)

    def spread(buf, core, s, r, f_s, f_r):
        own = buf.at[chip, core]
        forwards = {0: remote(own, own, f_s.at[0], f_r.at[0], sibling)}
        sends = {k: remote(own, own, s.at[k], r.at[k], plane[k]) for k in SPREAD}
        for d in [*sends.values(), forwards[0]]:
            d.start()
        return sends, forwards

    def forward(buf, core, sends, forwards, order, f_s, f_r):
        for k in order:
            sends[k].wait_recv()
            got = buf.at[plane_from[k], 1 - core]
            forwards[k] = remote(got, got, f_s.at[k], f_r.at[k], sibling)
            forwards[k].start()

    def merge(buf, pair):
        half = (x // 2) ^ pair
        forwards = v_forwards if buf is vb else u_forwards
        for k in range(pair * 8, pair * 8 + 8):
            forwards[k].wait_recv()
        total = jnp.zeros((8, ROWS), F32)
        for j in range(8):
            base = j * CHIP
            got = buf.at[half * 8 + j]
            nat[base : base + 160] = got[0, 0:160]
            e0 = got[0, 160:176].astype(F32)
            e1 = got[1, 0:16].astype(F32)
            edge = jnp.concatenate([e0[:8], e1[8:]], axis=0)
            nat[base + 160 : base + 176] = edge.astype(BF16)
            nat[base + 176 : base + 336] = got[1, 16:176]
            total = total + (e0[8:] + e1[:8])
        return total

    def product(acc, pair, tiles):
        cols = pl.ds(pl.multiple_of(((x // 2) ^ pair) * HALF, 128), HALF)
        for m in tiles:
            rows = pl.ds(m * 256, 256)
            t = jnp.dot(l_v[rows, cols], nat[...], preferred_element_type=F32)
            acc[rows] = t if pair == FIRST else acc[rows] + t

    ins[0].wait()
    ins[1].wait()
    part[:COLS] = lax.dot_general(
        w_v[...], a_v[...], (((1,), (1,)), ((), ())), preferred_element_type=F32
    )
    part[COLS:] = jnp.zeros((8 * CHUNK - COLS, ROWS), F32)
    pl.semaphore_wait(barrier, 30 + 15 * c)
    rs_sends = {}
    for k in ZLINE:
        chunk = part.at[pl.ds(pl.multiple_of((z + k) % 8 * CHUNK, 8), CHUNK)]
        rs_sends[k] = remote(chunk, rs.at[k], rs_s.at[k], rs_r.at[k], zline[k])
        rs_sends[k].start()

    for i in (2, 3, 4):
        ins[i].wait()
    skip_t[...] = column(skip_v[...].astype(F32))
    g1_t[...] = column(1.0 + jnp.broadcast_to(g1_v[...], (ROWS, COLS)))
    g2_t[...] = column(1.0 + jnp.broadcast_to(g2_v[...], (ROWS, COLS)))
    vb[chip, c] = framed(skip_t[...] * g2_t[...], jnp.zeros((8, ROWS), F32), c)
    v_sends, v_forwards = spread(vb, c, v_s, v_r, vf_s, vf_r)

    for i in (5, 6, 7, 8):
        ins[i].wait()
    block = (z * 32 + v) * VOC // BLOCK
    slot = lax.broadcasted_iota(jnp.int32, (NB, 64), 0)
    listed = []
    for s in range(2):
        hit = (ids_v[s] == block) & (slot < tot_v[s : s + 1])
        listed.append(jnp.max(jnp.where(hit, 1.0, 0.0), axis=0, keepdims=True))
    banned = jnp.concatenate(listed, axis=1)
    fed = jnp.where((sub_v[...] >> 11) == block, 1.0, 0.0)
    fed = jnp.concatenate([jnp.zeros((1, 64), F32), fed], axis=1)
    info[0:1] = jnp.maximum(banned, fed)
    warm = warm_v[...]
    info[1:2] = 1.0 / jnp.concatenate([warm[0:1], warm[1:2]], axis=1)

    total = jnp.zeros((CHUNK, ROWS), F32)
    for k in reversed(ZLINE):
        rs_sends[k].wait_recv()
        total = total + rs[k]
    sums[...] = total
    zb_sends = []
    for k in ZLINE:
        chunk = zb.at[pl.ds(pl.multiple_of(z * CHUNK, 8), CHUNK)]
        zb_sends.append(remote(sums, chunk, zb_s.at[k], zb_r.at[k], zline[k]))
        zb_sends[-1].start()
    for d in reversed(zb_sends):
        d.wait_recv()
    p = zb[:COLS]
    skip = skip_t[...]
    gained = p * g1_t[...]
    stats = [
        jnp.sum(t, axis=0, keepdims=True) for t in (p * p, skip * skip, skip * gained, gained * gained)
    ]
    hi, lo = split16(jnp.concatenate(stats, axis=0))
    ub[chip, c] = framed(gained * g2_t[...], jnp.concatenate([hi, lo], axis=0), c)
    u_sends, u_forwards = spread(ub, c, u_s, u_r, uf_s, uf_r)

    forward(vb, c, v_sends, v_forwards, SPREAD, vf_s, vf_r)
    for d in l_in:
        d.wait()
    for pair in (FIRST, 1 - FIRST):
        merge(vb, pair)
        product(vacc, pair, range(4))
    forward(ub, c, u_sends, u_forwards, SPREAD, uf_s, uf_r)
    stat[...] = merge(ub, 0)
    product(uacc, 0, range(4))
    stat[...] += merge(ub, 1)
    total = stat[:4] + stat[4:]
    r1 = lax.rsqrt(total[0:1] / D + EPS)
    square = total[1:2] + 2.0 * r1 * total[2:3] + r1 * r1 * total[3:4]
    r2 = lax.rsqrt(jnp.maximum(square, 0.0) / D + EPS)
    warmth = r2 * info[1:2]
    banned = info[0:1]
    cols = pl.ds(pl.multiple_of((1 - x // 2) * HALF, 128), HALF)
    peaks, masses = [], []
    for m in range(4):
        rows = pl.ds(m * 256, 256)
        t = jnp.dot(l_v[rows, cols], nat[...], preferred_element_type=F32)
        t = (vacc[rows] + r1 * (uacc[rows] + t)) * warmth
        vacc[rows] = t
        peaks.append(jnp.max(t, axis=0, keepdims=True))
        masses.append(jnp.sum(jnp.exp(t - peaks[m]), axis=0, keepdims=True))
    peak = functools.reduce(jnp.maximum, peaks)
    mass = sum(w * jnp.exp(q - peak) for w, q in zip(masses, peaks))
    lse = jnp.where(banned > 0.0, -1e30, peak + jnp.log(mass))

    def sent(*groups):
        for group in groups:
            for d in group:
                d.wait_send()

    def logsum(values):
        top = functools.reduce(jnp.maximum, values)
        return top + jnp.log(sum(jnp.exp(q - top) for q in values))

    la[32] = lse
    la_sends = {
        k: remote(la.at[32], la.at[2 * k + c], la_s.at[k], la_r.at[2 * k + c], place(z, x ^ (k // 4), y ^ (k % 4), 1))
        for k in PLANE + (0,)
    }
    for k in PLANE:
        la_sends[k].start()
    pl.when(c == 0)(la_sends[0].start)
    for m in range(8):
        t = vacc[pl.ds(m * 128, 128)]
        out_v[:, pl.ds(m * 128, 128)] = jnp.where(banned > 0.0, -30.0, t).T
    out_copy = copy_in(out_v, scaled_hbm, out_sem.at[0])
    sent(v_sends.values(), v_forwards.values(), rs_sends.values(), zb_sends)
    lb_sends = {
        k: remote(lb.at[8], lb.at[k // 2], lb_s.at[k], lb_r.at[k // 2], place((z + k // 2) % 8, x, y, 1 - k % 2))
        for k in ZBOTH
    }

    @pl.when(c == 1)
    def _():
        for k in (0,) + PLANE[::-1]:
            for core in (1, 0) if k else (0,):
                remote(la.at[32], la.at[2 * k + core], la_s.at[k], la_r.at[2 * k + core], sibling).wait_recv()
        lb[8] = logsum([la[j] for j in range(32) if j != 1] + [lse])
        for k in ZBOTH:
            lb_sends[k].start()
        lb[0] = lb[8]

    sent(u_sends.values(), u_forwards.values(), [la_sends[k] for k in PLANE])
    pl.when(c == 0)(la_sends[0].wait_send)
    pl.when(c == 0)(remote(lb.at[8], lb.at[0], lb_s.at[1], lb_r.at[0], sibling).wait_recv)
    for k in (1, 7, 2, 6, 3, 5, 4):
        remote(lb.at[8], lb.at[k], lb_s.at[2 * k], lb_r.at[k], sibling).wait_recv()
    lse = logsum([lb[k] for k in range(8)])
    shift_v[...] = jnp.where(banned > 0.0, 0.0, lse)
    shift_copy = copy_in(shift_v, shift_hbm, out_sem.at[1])

    @pl.when(c == 1)
    def _():
        sent(lb_sends.values())

    out_copy.wait()
    shift_copy.wait()


def local(a, w, g1, skip, g2, lexicon, warm, ids, total, sub):
    dma = pltpu.SemaphoreType.DMA
    vm = pltpu.VMEM
    scaled, shift = pl.pallas_call(
        kernel,
        name="head",
        out_shape=(
            jax.ShapeDtypeStruct((ROWS, VOC), F32),
            jax.ShapeDtypeStruct((1, ROWS), F32),
        ),
        in_specs=[pl.BlockSpec(memory_space=pl.ANY)] * 10,
        out_specs=(pl.BlockSpec(memory_space=pl.ANY),) * 2,
        scratch_shapes=[
            vm((ROWS, 2688), BF16),
            vm((COLS, 2688), BF16),
            vm((1, COLS), F32),
            vm((ROWS, COLS), BF16),
            vm((1, COLS), F32),
            vm((VOC, D), BF16),
            vm((2, 64), F32),
            vm((2, NB, 64), jnp.int32),
            vm((2, 64), jnp.int32),
            vm((1, 64), jnp.int32),
        ]
        + [vm((COLS, ROWS), F32)] * 3
        + [
            vm((8 * CHUNK, ROWS), F32),
            vm((8, CHUNK, ROWS), F32),
            vm((CHUNK, ROWS), F32),
            vm((8 * CHUNK, ROWS), F32),
            vm((16, 2, PART, ROWS), BF16),
            vm((16, 2, PART, ROWS), BF16),
            vm((HALF, ROWS), BF16),
            vm((VOC, ROWS), F32),
            vm((VOC, ROWS), F32),
            vm((ROWS, VOC), F32),
            vm((1, ROWS), F32),
            vm((33, 1, ROWS), F32),
            vm((9, 1, ROWS), F32),
            vm((8, ROWS), F32),
            vm((8, ROWS), F32),
            dma((9,)),
            dma((4,)),
        ]
        + [dma((8,))] * 4
        + [dma((16,))] * 8
        + [dma((16,)), dma((32,)), dma((16,)), dma((8,))]
        + [dma((2,))],
        compiler_params=pltpu.CompilerParams(
            collective_id=0, has_side_effects=True, vmem_limit_bytes=63 * 1024 * 1024
        ),
    )(
        a.reshape(ROWS, 2688),
        w.T,
        g1.reshape(1, COLS),
        skip.reshape(ROWS, COLS),
        g2.reshape(1, COLS),
        lexicon,
        warm,
        ids.transpose(0, 2, 1),
        total,
        sub.reshape(1, 64),
    )
    return (scaled - shift.reshape(ROWS, 1)).reshape(2, 64, VOC)


def solution(mesh):
    placed = (
        P(None, None, "tensor"),
        P("tensor", "vocab"),
        P("vocab"),
        P(None, None, "vocab"),
        P("vocab"),
        P(("tensor", "vocab"), None),
        P(),
        P(),
        P(),
        P(),
    )
    return jax.shard_map(
        local,
        mesh=mesh,
        in_specs=placed,
        out_specs=P(None, None, ("tensor", "vocab")),
        check_vma=False,
    )
```

```python
import functools

import jax
import jax.numpy as jnp
from jax import lax
from jax.experimental import pallas as pl
from jax.experimental.pallas import tpu as pltpu
from jax.sharding import PartitionSpec as P

BLOCK = 2048
NB = 16
ROWS = 128
D = 5376
COLS = 168
CHUNK = 24
PART = 176
CHIP = 336
VOC = 1024
HALF = D // 2
MESH = pl.DeviceIdType.MESH
ZLINE = (4, 3, 5, 2, 6, 1, 7, 0)
ZBOTH = (8, 9, 6, 7, 10, 11, 4, 5, 12, 13, 2, 3, 14, 15, 1)
SPREAD = (10, 11, 9, 14, 6, 8, 13, 15, 12, 2, 5, 7, 4, 1, 3)
FIRST = 1
PLANE = (10, 11, 9, 6, 14, 2, 8, 5, 7, 13, 15, 1, 3, 4, 12)
F32, BF16 = jnp.float32, jnp.bfloat16
EPS = 1e-6


def place(z, x, y, c):
    return (z, (x * 4 + y) * 2 + c)


def split16(s):
    hi = s.astype(BF16).astype(F32)
    return hi, (s - hi)


def column(value):
    n = value.shape[0]
    wide = jnp.concatenate([value, jnp.zeros((n, 256 - COLS), F32)], axis=1)
    return wide.T[:COLS]


def kernel(
    a_hbm, w_hbm, g1_hbm, skip_hbm, g2_hbm, l_hbm, warm_hbm, ids_hbm, tot_hbm, sub_hbm,
    scaled_hbm, shift_hbm,
    a_v, w_v, g1_v, skip_v, g2_v, l_v, warm_v, ids_v, tot_v, sub_v,
    skip_t, g1_t, g2_t, part, rs, sums, zb, ub, vb, nat, uacc, vacc, out_v, shift_v, la, lb, info, stat,
    in_sem, l_sem, rs_s, rs_r, zb_s, zb_r, u_s, u_r, v_s, v_r, uf_s, uf_r, vf_s, vf_r,
    la_s, la_r, lb_s, lb_r, out_sem,
):
    z = lax.axis_index("tensor")
    v = lax.axis_index("vocab")
    x, y, c = v // 8, (v // 2) % 4, v % 2
    chip = x * 4 + y
    other = 1 - c

    def copy_in(src, dst, sem):
        d = pltpu.make_async_copy(src, dst, sem)
        d.start()
        return d

    def remote(src, dst, s, r, to):
        return pltpu.make_async_remote_copy(src, dst, s, r, device_id=to, device_id_type=MESH)

    pairs = [
        (a_hbm, a_v), (w_hbm, w_v), (skip_hbm, skip_v), (g1_hbm, g1_v), (g2_hbm, g2_v),
        (warm_hbm, warm_v), (ids_hbm, ids_v), (tot_hbm, tot_v), (sub_hbm, sub_v),
    ]
    zline = [place((z + k) % 8, x, y, other) for k in range(8)]
    plane = [place(z, x ^ (k // 4), y ^ (k % 4), other) for k in range(16)]
    plane_from = [(x ^ (k // 4)) * 4 + (y ^ (k % 4)) for k in range(16)]
    zboth = [place((z + k // 2) % 8, x, y, (c + k % 2) % 2) for k in range(16)]
    sibling = plane[0]

    ins = [copy_in(s, d, in_sem.at[i]) for i, (s, d) in enumerate(pairs[:2])]
    barrier = pltpu.get_barrier_semaphore()
    for peer in [zboth[k] for k in ZBOTH] + [plane[k] for k in PLANE]:
        pl.semaphore_signal(barrier, inc=1, device_id=peer, device_id_type=MESH)

    @pl.when(c == 1)
    def _():
        for k in PLANE:
            to = place(z, x ^ (k // 4), y ^ (k % 4), 1)
            pl.semaphore_signal(barrier, inc=1, device_id=to, device_id_type=MESH)

    ins += [copy_in(s, d, in_sem.at[i + 2]) for i, (s, d) in enumerate(pairs[2:])]
    l_in = [
        copy_in(l_hbm.at[pl.ds(i * 256, 256)], l_v.at[pl.ds(i * 256, 256)], l_sem.at[i])
        for i in range(4)
    ]

    def framed(body, extra, core):
        low = jnp.concatenate([body, extra], axis=0)
        high = jnp.concatenate([extra, body], axis=0)
        return jnp.where(core == 0, low, high).astype(BF16)

    def spread(buf, core, s, r, f_s, f_r):
        own = buf.at[chip, core]
        forwards = {0: remote(own, own, f_s.at[0], f_r.at[0], sibling)}
        sends = {k: remote(own, own, s.at[k], r.at[k], plane[k]) for k in SPREAD}
        for d in [*sends.values(), forwards[0]]:
            d.start()
        return sends, forwards

    def forward(buf, core, sends, forwards, order, f_s, f_r):
        for k in order:
            sends[k].wait_recv()
            got = buf.at[plane_from[k], 1 - core]
            forwards[k] = remote(got, got, f_s.at[k], f_r.at[k], sibling)
            forwards[k].start()

    def merge(buf, pair):
        half = (x // 2) ^ pair
        forwards = v_forwards if buf is vb else u_forwards
        for k in range(pair * 8, pair * 8 + 8):
            forwards[k].wait_recv()
        total = jnp.zeros((8, ROWS), F32)
        for j in range(8):
            base = j * CHIP
            got = buf.at[half * 8 + j]
            nat[base : base + 160] = got[0, 0:160]
            e0 = got[0, 160:176].astype(F32)
            e1 = got[1, 0:16].astype(F32)
            edge = jnp.concatenate([e0[:8], e1[8:]], axis=0)
            nat[base + 160 : base + 176] = edge.astype(BF16)
            nat[base + 176 : base + 336] = got[1, 16:176]
            total = total + (e0[8:] + e1[:8])
        return total

    def product(acc, pair, tiles):
        cols = pl.ds(pl.multiple_of(((x // 2) ^ pair) * HALF, 128), HALF)
        for m in tiles:
            rows = pl.ds(m * 256, 256)
            t = jnp.dot(l_v[rows, cols], nat[...], preferred_element_type=F32)
            acc[rows] = t if pair == FIRST else acc[rows] + t

    ins[0].wait()
    ins[1].wait()
    part[:COLS] = lax.dot_general(
        w_v[...], a_v[...], (((1,), (1,)), ((), ())), preferred_element_type=F32
    )
    part[COLS:] = jnp.zeros((8 * CHUNK - COLS, ROWS), F32)
    pl.semaphore_wait(barrier, 30 + 15 * c)
    rs_sends = {}
    for k in ZLINE:
        chunk = part.at[pl.ds(pl.multiple_of((z + k) % 8 * CHUNK, 8), CHUNK)]
        rs_sends[k] = remote(chunk, rs.at[k], rs_s.at[k], rs_r.at[k], zline[k])
        rs_sends[k].start()

    for i in (2, 3, 4):
        ins[i].wait()
    skip_t[...] = column(skip_v[...].astype(F32))
    g1_t[...] = column(1.0 + jnp.broadcast_to(g1_v[...], (ROWS, COLS)))
    g2_t[...] = column(1.0 + jnp.broadcast_to(g2_v[...], (ROWS, COLS)))
    vb[chip, c] = framed(skip_t[...] * g2_t[...], jnp.zeros((8, ROWS), F32), c)
    v_sends, v_forwards = spread(vb, c, v_s, v_r, vf_s, vf_r)

    for i in (5, 6, 7, 8):
        ins[i].wait()
    block = (z * 32 + v) * VOC // BLOCK
    slot = lax.broadcasted_iota(jnp.int32, (NB, 64), 0)
    listed = []
    for s in range(2):
        hit = (ids_v[s] == block) & (slot < tot_v[s : s + 1])
        listed.append(jnp.max(jnp.where(hit, 1.0, 0.0), axis=0, keepdims=True))
    banned = jnp.concatenate(listed, axis=1)
    fed = jnp.where((sub_v[...] >> 11) == block, 1.0, 0.0)
    fed = jnp.concatenate([jnp.zeros((1, 64), F32), fed], axis=1)
    info[0:1] = jnp.maximum(banned, fed)
    warm = warm_v[...]
    info[1:2] = 1.0 / jnp.concatenate([warm[0:1], warm[1:2]], axis=1)

    total = jnp.zeros((CHUNK, ROWS), F32)
    for k in reversed(ZLINE):
        rs_sends[k].wait_recv()
        total = total + rs[k]
    sums[...] = total
    zb_sends = []
    for k in ZLINE:
        chunk = zb.at[pl.ds(pl.multiple_of(z * CHUNK, 8), CHUNK)]
        zb_sends.append(remote(sums, chunk, zb_s.at[k], zb_r.at[k], zline[k]))
        zb_sends[-1].start()
    for d in reversed(zb_sends):
        d.wait_recv()
    p = zb[:COLS]
    skip = skip_t[...]
    gained = p * g1_t[...]
    stats = [
        jnp.sum(t, axis=0, keepdims=True) for t in (p * p, skip * skip, skip * gained, gained * gained)
    ]
    hi, lo = split16(jnp.concatenate(stats, axis=0))
    ub[chip, c] = framed(gained * g2_t[...], jnp.concatenate([hi, lo], axis=0), c)
    u_sends, u_forwards = spread(ub, c, u_s, u_r, uf_s, uf_r)

    forward(vb, c, v_sends, v_forwards, SPREAD, vf_s, vf_r)
    for d in l_in:
        d.wait()
    for pair in (FIRST, 1 - FIRST):
        merge(vb, pair)
        product(vacc, pair, range(4))
    forward(ub, c, u_sends, u_forwards, SPREAD, uf_s, uf_r)
    stat[...] = merge(ub, 1)
    product(uacc, 1, range(4))
    stat[...] += merge(ub, 0)
    total = stat[:4] + stat[4:]
    r1 = lax.rsqrt(total[0:1] / D + EPS)
    square = total[1:2] + 2.0 * r1 * total[2:3] + r1 * r1 * total[3:4]
    r2 = lax.rsqrt(jnp.maximum(square, 0.0) / D + EPS)
    warmth = r2 * info[1:2]
    banned = info[0:1]
    cols = pl.ds(pl.multiple_of(x // 2 * HALF, 128), HALF)
    peaks, masses = [], []
    for m in range(4):
        rows = pl.ds(m * 256, 256)
        t = jnp.dot(l_v[rows, cols], nat[...], preferred_element_type=F32)
        t = (vacc[rows] + r1 * (uacc[rows] + t)) * warmth
        vacc[rows] = t
        peaks.append(jnp.max(t, axis=0, keepdims=True))
        masses.append(jnp.sum(jnp.exp(t - peaks[m]), axis=0, keepdims=True))
    peak = functools.reduce(jnp.maximum, peaks)
    mass = sum(w * jnp.exp(q - peak) for w, q in zip(masses, peaks))
    lse = jnp.where(banned > 0.0, -1e30, peak + jnp.log(mass))

    def sent(*groups):
        for group in groups:
            for d in group:
                d.wait_send()

    def logsum(values):
        top = functools.reduce(jnp.maximum, values)
        return top + jnp.log(sum(jnp.exp(q - top) for q in values))

    la[32] = lse
    la_sends = {
        k: remote(la.at[32], la.at[2 * k + c], la_s.at[k], la_r.at[2 * k + c], place(z, x ^ (k // 4), y ^ (k % 4), 1))
        for k in PLANE + (0,)
    }
    for k in PLANE:
        la_sends[k].start()
    pl.when(c == 0)(la_sends[0].start)
    for m in range(8):
        t = vacc[pl.ds(m * 128, 128)]
        out_v[:, pl.ds(m * 128, 128)] = jnp.where(banned > 0.0, -30.0, t).T
    out_copy = copy_in(out_v, scaled_hbm, out_sem.at[0])
    sent(v_sends.values(), v_forwards.values(), rs_sends.values(), zb_sends)
    lb_sends = {
        k: remote(lb.at[8], lb.at[k // 2], lb_s.at[k], lb_r.at[k // 2], place((z + k // 2) % 8, x, y, 1 - k % 2))
        for k in ZBOTH
    }

    @pl.when(c == 1)
    def _():
        for k in (0,) + PLANE[::-1]:
            for core in (1, 0) if k else (0,):
                remote(la.at[32], la.at[2 * k + core], la_s.at[k], la_r.at[2 * k + core], sibling).wait_recv()
        lb[8] = logsum([la[j] for j in range(32) if j != 1] + [lse])
        for k in ZBOTH:
            lb_sends[k].start()
        lb[0] = lb[8]

    sent(u_sends.values(), u_forwards.values(), [la_sends[k] for k in PLANE])
    pl.when(c == 0)(la_sends[0].wait_send)
    pl.when(c == 0)(remote(lb.at[8], lb.at[0], lb_s.at[1], lb_r.at[0], sibling).wait_recv)
    for k in (1, 7, 2, 6, 3, 5, 4):
        remote(lb.at[8], lb.at[k], lb_s.at[2 * k], lb_r.at[k], sibling).wait_recv()
    lse = logsum([lb[k] for k in range(8)])
    shift_v[...] = jnp.where(banned > 0.0, 0.0, lse)
    shift_copy = copy_in(shift_v, shift_hbm, out_sem.at[1])

    @pl.when(c == 1)
    def _():
        sent(lb_sends.values())

    out_copy.wait()
    shift_copy.wait()


def local(a, w, g1, skip, g2, lexicon, warm, ids, total, sub):
    dma = pltpu.SemaphoreType.DMA
    vm = pltpu.VMEM
    scaled, shift = pl.pallas_call(
        kernel,
        name="head",
        out_shape=(
            jax.ShapeDtypeStruct((ROWS, VOC), F32),
            jax.ShapeDtypeStruct((1, ROWS), F32),
        ),
        in_specs=[pl.BlockSpec(memory_space=pl.ANY)] * 10,
        out_specs=(pl.BlockSpec(memory_space=pl.ANY),) * 2,
        scratch_shapes=[
            vm((ROWS, 2688), BF16),
            vm((COLS, 2688), BF16),
            vm((1, COLS), F32),
            vm((ROWS, COLS), BF16),
            vm((1, COLS), F32),
            vm((VOC, D), BF16),
            vm((2, 64), F32),
            vm((2, NB, 64), jnp.int32),
            vm((2, 64), jnp.int32),
            vm((1, 64), jnp.int32),
        ]
        + [vm((COLS, ROWS), F32)] * 3
        + [
            vm((8 * CHUNK, ROWS), F32),
            vm((8, CHUNK, ROWS), F32),
            vm((CHUNK, ROWS), F32),
            vm((8 * CHUNK, ROWS), F32),
            vm((16, 2, PART, ROWS), BF16),
            vm((16, 2, PART, ROWS), BF16),
            vm((HALF, ROWS), BF16),
            vm((VOC, ROWS), F32),
            vm((VOC, ROWS), F32),
            vm((ROWS, VOC), F32),
            vm((1, ROWS), F32),
            vm((33, 1, ROWS), F32),
            vm((9, 1, ROWS), F32),
            vm((8, ROWS), F32),
            vm((8, ROWS), F32),
            dma((9,)),
            dma((4,)),
        ]
        + [dma((8,))] * 4
        + [dma((16,))] * 8
        + [dma((16,)), dma((32,)), dma((16,)), dma((8,))]
        + [dma((2,))],
        compiler_params=pltpu.CompilerParams(
            collective_id=0, has_side_effects=True, vmem_limit_bytes=63 * 1024 * 1024
        ),
    )(
        a.reshape(ROWS, 2688),
        w.T,
        g1.reshape(1, COLS),
        skip.reshape(ROWS, COLS),
        g2.reshape(1, COLS),
        lexicon,
        warm,
        ids.transpose(0, 2, 1),
        total,
        sub.reshape(1, 64),
    )
    return (scaled - shift.reshape(ROWS, 1)).reshape(2, 64, VOC)


def solution(mesh):
    placed = (
        P(None, None, "tensor"),
        P("tensor", "vocab"),
        P("vocab"),
        P(None, None, "vocab"),
        P("vocab"),
        P(("tensor", "vocab"), None),
        P(),
        P(),
        P(),
        P(),
    )
    return jax.shard_map(
        local,
        mesh=mesh,
        in_specs=placed,
        out_specs=P(None, None, ("tensor", "vocab")),
        check_vma=False,
    )
```
